32 devices in a mesh: groups: 2 (over y), blk: 4 (over z), dim: 2 (over x), rep: 2 (over core).
Axes of the slice: x: 2, y: 2, z: 4, core: 2. Of those that a mesh axis runs over, the one named last changes fastest.
Arguments:
- train_grads: bfloat16 [8192, 8192], P(('groups', 'blk'), 'dim'), parts along dimension 0, may hold values from -6 to 6
- query_grads: bfloat16 [2048, 8192], P(('groups', 'rep', 'blk'), 'dim'), parts along dimension 0, may hold values from -0.0625 to 0.0625
- precond: float32 [8192], P('dim'), may hold values from 0.1 to 1
- candidates: int32 [64, 8], P(('groups', 'blk'), 'rep'), parts along dimension 0, may hold values from 0 to 1, as said below
Outputs:
- scores: float32 [8192, 1024], P(('groups', 'blk', 'dim'), 'rep'), parts along dimension 0
The draws below stay inside these ranges and needn't reach their ends.
There are 2 independent parts, one for each index of `groups`. The reference program is written for one: setup_inputs(seed, part) draws one part's arguments, and reference() takes and returns one part's arrays. A program takes and returns all parts, laid end to end along the dimension named above; an argument that names none is the same for every part. Nothing has to cross between parts.
Inputs may be any that keep to these rules, and one draw needn't show every extreme that they name: `candidates`: each index of blk holds its tiles' entries with its own density, drawn from eighths of one to one.
All inputs are finite; a program needn't handle non-finite values.
Results may differ from the reference program's by a relative error of at most 0.0029.
Values may be sent and summed in bfloat16 or wider, within the bound.
A program may use at most 128 MiB of HBM per device.

```python
import math
import jax
import jax.numpy as jnp
from jax import lax

K = 8192
NT_DEV = 1024
QB = 128
TILE = 128
N_TRAIN = 4096
N_QBLK = 8
QTOT = 1024
N_TILES = 32


def draw_candidates(key, part):
    key = jax.random.fold_in(key, 7)
    level_key, bits_key = jax.random.split(key)
    shards = N_TILES // (NT_DEV // TILE)
    levels = jax.random.randint(level_key, (shards,), 1, 9)
    owner = jnp.arange(N_TILES) // (NT_DEV // TILE)
    bits = jax.random.randint(bits_key, (N_TILES, N_QBLK), 0, 8)
    return (bits < levels[owner][:, None]).astype(jnp.int32)


def block_scale(own_key, dims, pieces, smallest, high):
    def one(axis_at, parts):
        steps = jax.random.uniform(jax.random.fold_in(jax.random.fold_in(own_key, 6), axis_at), (parts,), jnp.float32, smallest / len(pieces), high / len(pieces))
        return jnp.repeat(jnp.exp(steps), dims[axis_at] // parts).reshape((-1,) + (1,) * (len(dims) - axis_at - 1))

    gain = one(*pieces[0])
    for cut in pieces[1:]:
        gain = gain * one(*cut)
    return gain


def noise(rng, dims, spread, most, cuts=(), kind=jnp.bfloat16):
    result = spread * jax.random.normal(rng, dims, jnp.float32)
    if cuts:
        result = result * block_scale(rng, dims, cuts, -0.22, 0.18)
    return jnp.clip(result, -most, most).astype(kind)


def setup_inputs(seed: int = 0, part: int = 0) -> dict:
    arg_keys = jax.random.split(jax.random.key(seed), 5)
    part_splits = jax.random.split(jax.random.fold_in(arg_keys[4], part), 5)
    return {
        "train_grads": noise(part_splits[0], (N_TRAIN, K), 1.0, 6.0, ((0, 4), (1, 2))),
        "query_grads": noise(part_splits[1], (QTOT, K), K ** -0.5, 0.0625, ((0, 8), (1, 2))),
        "precond": jnp.clip(jnp.exp(math.log(1.0) - 2.3025851 * jax.random.uniform(arg_keys[2], (K,), jnp.float32) ** block_scale(arg_keys[2], (K,), ((0, 2),), -0.2, 0.2)), 0.1, 1.0),
        "candidates": draw_candidates(jax.random.fold_in(jax.random.fold_in(arg_keys[4], part), 71), part),
    }


def reference(train_grads, query_grads, precond, candidates):
    prepared = (query_grads.astype(jnp.float32) * lax.rsqrt(precond)[None, :]).astype(jnp.bfloat16)
    blocks = prepared.reshape(QTOT // QB, QB, K)

    def one_block(block):
        return jnp.dot(train_grads, block.T, preferred_element_type=jnp.float32)
    raw = lax.map(one_block, blocks)
    raw = jnp.transpose(raw, (1, 0, 2))
    keep = candidates.astype(jnp.float32)
    masked = raw.reshape(N_TRAIN // TILE, TILE, QTOT // QB, QB) * keep[:, None, :, None]
    return masked.reshape(N_TRAIN, QTOT)
```

```python
import functools

import jax
import jax.numpy as jnp
from jax import lax
from jax.experimental import pallas as pl
from jax.experimental.pallas import tpu as pltpu
from jax.sharding import PartitionSpec as P

MESH = pl.DeviceIdType.MESH


def kernel(
    nb, nd, query, precond, keep, train_hbm, own_hbm, got_hbm,
    train, held, acc_hi, acc_lo, out_buf, part_buf,
    train_sem, send_lo, send_hi, recv, part_send, part_recv, own_sem,
):
    chunks, rows, depth = train.shape
    width = held.shape[2]
    half = rows // nd
    tiles = keep.shape[0]
    tile = rows // tiles
    z = lax.axis_index("blk")
    x = lax.axis_index("dim")
    has_lo = z > 0
    has_hi = z < nb - 1
    barrier = pltpu.get_barrier_semaphore()

    @pl.when(has_lo)
    def _():
        pl.semaphore_signal(barrier, inc=1, device_id={"blk": z - 1}, device_id_type=MESH)

    @pl.when(has_hi)
    def _():
        pl.semaphore_signal(barrier, inc=1, device_id={"blk": z + 1}, device_id_type=MESH)

    for d in range(1, nd):
        pl.semaphore_signal(
            barrier, inc=1, device_id={"dim": lax.rem(x + d, nd)}, device_id_type=MESH
        )

    def load(c):
        return pltpu.make_async_copy(
            train_hbm.at[:, pl.ds(c * depth, depth)], train.at[c], train_sem.at[c]
        )

    for c in range(chunks):
        load(c).start()

    def to_lo(b, c):
        return pltpu.make_async_remote_copy(
            src_ref=held.at[b, c], dst_ref=held.at[b, c],
            send_sem=send_lo.at[b, c], recv_sem=recv.at[b, c],
            device_id={"blk": z - 1}, device_id_type=MESH,
        )

    def to_hi(b, c):
        return pltpu.make_async_remote_copy(
            src_ref=held.at[b, c], dst_ref=held.at[b, c],
            send_sem=send_hi.at[b, c], recv_sem=recv.at[b, c],
            device_id={"blk": z + 1}, device_id_type=MESH,
        )

    def prepare(c):
        span = slice(c * depth, (c + 1) * depth)
        scale = lax.rsqrt(precond[:, span])
        held[z, c] = (query[:, span].astype(jnp.float32) * scale).astype(jnp.bfloat16)

    prepare(0)
    between = has_lo & has_hi

    @pl.when(between)
    def _():
        pl.semaphore_wait(barrier, nd + 1)

    @pl.when(jnp.logical_not(between))
    def _():
        pl.semaphore_wait(barrier, nd)

    for c in range(chunks):
        if c:
            prepare(c)

        @pl.when(has_lo)
        def _():
            to_lo(z, c).start()

        @pl.when(has_hi)
        def _():
            to_hi(z, c).start()

    def add_chunk(acc, b, c):
        block = held[b, c]

        def one(i, carry):
            at = pl.ds(pl.multiple_of(i * 256, 256), 256)
            value = lax.dot_general(
                train[c, at, :], block, (((1,), (1,)), ((), ())),
                preferred_element_type=jnp.float32,
            )

            @pl.when(c == 0)
            def _():
                acc[at, :] = value

            @pl.when(c > 0)
            def _():
                acc[at, :] += value

            return carry

        lax.fori_loop(0, rows // 256, one, 0)

    def part_copy(b, d):
        return pltpu.make_async_remote_copy(
            src_ref=part_buf.at[d - 1, b],
            dst_ref=got_hbm.at[d - 1, :, pl.ds(pl.multiple_of(b * width, width), width)],
            send_sem=part_send.at[d - 1, b], recv_sem=part_recv.at[d - 1, b],
            device_id={"dim": lax.rem(x + d, nd)}, device_id_type=MESH,
        )

    def own_copy(b):
        return pltpu.make_async_copy(
            out_buf.at[b],
            own_hbm.at[:, pl.ds(pl.multiple_of(b * width, width), width)],
            own_sem.at[b],
        )

    def masked(acc, b, first):
        values = []
        for i in range(half // tile):
            t = first * (half // tile) + i
            at = pl.ds(pl.multiple_of(t * tile, tile), tile)
            values.append(acc[at, :] * keep[t, b].astype(jnp.float32))
        return values

    def finish(acc, b):
        for d in range(1, nd):
            for i, value in enumerate(masked(acc, b, lax.rem(x + d, nd))):
                part_buf[d - 1, b, i * tile : (i + 1) * tile, :] = value.astype(jnp.bfloat16)
            part_copy(b, d).start()
        for i, value in enumerate(masked(acc, b, x)):
            out_buf[b, i * tile : (i + 1) * tile, :] = value
        own_copy(b).start()

    for c in range(chunks):
        load(c).wait()

    def own_chunk(c, carry):
        add_chunk(acc_hi, z, c)
        return carry

    lax.fori_loop(0, chunks, own_chunk, 0)
    finish(acc_hi, z)

    def step(s, carry):
        hi, lo = z + s, z - s

        def chunk(c, carry):
            @pl.when(hi < nb)
            def _():
                to_lo(hi, c).wait_recv()

                @pl.when(has_lo)
                def _():
                    to_lo(hi, c).start()

            @pl.when(lo >= 0)
            def _():
                to_hi(lo, c).wait_recv()

                @pl.when(has_hi)
                def _():
                    to_hi(lo, c).start()

            @pl.when(hi < nb)
            def _():
                add_chunk(acc_hi, hi, c)

            @pl.when(lo >= 0)
            def _():
                add_chunk(acc_lo, lo, c)

            return carry

        lax.fori_loop(0, chunks, chunk, 0)

        @pl.when(hi < nb)
        def _():
            finish(acc_hi, hi)

        @pl.when(lo >= 0)
        def _():
            finish(acc_lo, lo)

        return carry

    lax.fori_loop(1, nb, step, 0)

    def drain(b, carry):
        def drain_chunk(c, carry):
            @pl.when(has_lo & (b >= z))
            def _():
                to_lo(b, c).wait_send()

            @pl.when(has_hi & (b <= z))
            def _():
                to_hi(b, c).wait_send()

            return carry

        lax.fori_loop(0, chunks, drain_chunk, 0)
        own_copy(b).wait()
        for d in range(1, nd):
            part_copy(b, d).wait()
        return carry

    lax.fori_loop(0, nb, drain, 0)


def body(train_grads, query_grads, precond, candidates):
    rows, depth = train_grads.shape
    width = query_grads.shape[0]
    nb, nd = lax.axis_size("blk"), lax.axis_size("dim")
    chunks = 4
    half = rows // nd
    own, got = pl.pallas_call(
        functools.partial(kernel, nb, nd),
        out_shape=(
            jax.ShapeDtypeStruct((half, nb * width), jnp.float32),
            jax.ShapeDtypeStruct((nd - 1, half, nb * width), jnp.bfloat16),
        ),
        in_specs=[
            pl.BlockSpec(memory_space=pltpu.VMEM),
            pl.BlockSpec(memory_space=pltpu.VMEM),
            pl.BlockSpec(memory_space=pltpu.SMEM),
            pl.BlockSpec(memory_space=pl.ANY),
        ],
        out_specs=(pl.BlockSpec(memory_space=pl.ANY), pl.BlockSpec(memory_space=pl.ANY)),
        scratch_shapes=[
            pltpu.VMEM((chunks, rows, depth // chunks), jnp.bfloat16),
            pltpu.VMEM((nb, chunks, width, depth // chunks), jnp.bfloat16),
            pltpu.VMEM((rows, width), jnp.float32),
            pltpu.VMEM((rows, width), jnp.float32),
            pltpu.VMEM((nb, half, width), jnp.float32),
            pltpu.VMEM((nd - 1, nb, half, width), jnp.bfloat16),
            pltpu.SemaphoreType.DMA((chunks,)),
            pltpu.SemaphoreType.DMA((nb, chunks)),
            pltpu.SemaphoreType.DMA((nb, chunks)),
            pltpu.SemaphoreType.DMA((nb, chunks)),
            pltpu.SemaphoreType.DMA((nd - 1, nb)),
            pltpu.SemaphoreType.DMA((nd - 1, nb)),
            pltpu.SemaphoreType.DMA((nb,)),
        ],
        compiler_params=pltpu.CompilerParams(
            collective_id=0, has_side_effects=True, vmem_limit_bytes=44 * 2**20
        ),
    )(query_grads, precond[None, :], candidates, train_grads)
    total = own
    for d in range(nd - 1):
        total = total + got[d].astype(jnp.float32)
    return total


def solution(mesh):
    in_specs = (
        P(("groups", "blk"), "dim"),
        P(("groups", "rep", "blk"), "dim"),
        P("dim"),
        P(("groups", "blk"), "rep"),
    )
    out_specs = P(("groups", "blk", "dim"), "rep")
    return jax.shard_map(body, mesh=mesh, in_specs=in_specs, out_specs=out_specs, check_vma=False)
```

```python
import functools

import jax
import jax.numpy as jnp
from jax import lax
from jax.experimental import pallas as pl
from jax.experimental.pallas import tpu as pltpu
from jax.sharding import PartitionSpec as P

MESH = pl.DeviceIdType.MESH


def kernel(
    nb, nd, nr, query, precond, keep, train_hbm, own_hbm, got_hbm,
    train, held, acc_hi, acc_lo, acc_off, out_buf, part_buf,
    end_train, end_own, end_part, end_got, end_sum, back,
    train_sem, send_lo, send_hi, recv, part_send, part_recv, own_sem,
    slice_send, slice_recv, twin_send, end_send, end_recv, back_send, back_recv,
):
    chunks, rows, depth = train.shape
    lent = end_train.shape[0]
    width = held.shape[2]
    half = rows // nd
    share = rows // nr
    tiles = keep.shape[0]
    tile = rows // tiles
    z = lax.axis_index("blk")
    x = lax.axis_index("dim")
    r = lax.axis_index("rep")
    has_lo = z > 0
    has_hi = z < nb - 1
    between = has_lo & has_hi
    is_end = jnp.logical_not(between)
    lo_host, hi_host = z == 1, z == nb - 2
    is_host = lo_host | hi_host
    outer = jnp.where(lo_host, 0, nb - 1)
    host = jnp.where(has_lo, nb - 2, 1)
    barrier = pltpu.get_barrier_semaphore()

    @pl.when(has_lo)
    def _():
        pl.semaphore_signal(barrier, inc=1, device_id={"blk": z - 1}, device_id_type=MESH)

    @pl.when(has_hi)
    def _():
        pl.semaphore_signal(barrier, inc=1, device_id={"blk": z + 1}, device_id_type=MESH)

    for d in range(1, nd):
        pl.semaphore_signal(
            barrier, inc=1, device_id={"dim": lax.rem(x + d, nd)}, device_id_type=MESH
        )
    for d in range(1, nr):
        pl.semaphore_signal(
            barrier, inc=1, device_id={"rep": lax.rem(r + d, nr)}, device_id_type=MESH
        )

    def load(c):
        return pltpu.make_async_copy(
            train_hbm.at[:, pl.ds(c * depth, depth)], train.at[c], train_sem.at[c]
        )

    for c in range(chunks):
        load(c).start()

    def to_lo(b, c):
        return pltpu.make_async_remote_copy(
            src_ref=held.at[b, c], dst_ref=held.at[b, c],
            send_sem=send_lo.at[b, c], recv_sem=recv.at[b, c],
            device_id={"blk": z - 1}, device_id_type=MESH,
        )

    def to_hi(b, c):
        return pltpu.make_async_remote_copy(
            src_ref=held.at[b, c], dst_ref=held.at[b, c],
            send_sem=send_hi.at[b, c], recv_sem=recv.at[b, c],
            device_id={"blk": z + 1}, device_id_type=MESH,
        )

    def goes_lo(c):
        return has_lo & ((z > 1) | (c >= lent))

    def goes_hi(c):
        return has_hi & ((z < nb - 2) | (c >= lent))

    def share_of(owner):
        return pl.ds(pl.multiple_of(owner * share, share), share)

    def slice_copy(c):
        return pltpu.make_async_remote_copy(
            src_ref=train.at[c, share_of(r), :], dst_ref=end_train.at[c, share_of(r), :],
            send_sem=slice_send.at[c], recv_sem=slice_recv.at[c, r],
            device_id={"blk": host}, device_id_type=MESH,
        )

    def twin_copy(c, d, owner):
        return pltpu.make_async_remote_copy(
            src_ref=end_train.at[c, share_of(owner), :],
            dst_ref=end_train.at[c, share_of(owner), :],
            send_sem=twin_send.at[c, d - 1], recv_sem=slice_recv.at[c, owner],
            device_id={"rep": lax.rem(r + d, nr)}, device_id_type=MESH,
        )

    def prepare(c):
        span = slice(c * depth, (c + 1) * depth)
        scale = lax.rsqrt(precond[:, span])
        held[z, c] = (query[:, span].astype(jnp.float32) * scale).astype(jnp.bfloat16)

    prepare(0)

    @pl.when(between)
    def _():
        pl.semaphore_wait(barrier, nd + nr)

    @pl.when(is_end)
    def _():
        pl.semaphore_wait(barrier, nd + nr - 1)

    for c in range(chunks):
        if c:
            prepare(c)
        if c == lent:

            @pl.when(is_end)
            def _():
                for e in range(lent):
                    load(e).wait()
                    slice_copy(e).start()

        @pl.when(goes_lo(c))
        def _():
            to_lo(z, c).start()

        @pl.when(goes_hi(c))
        def _():
            to_hi(z, c).start()

    def add_chunk(acc, source, b, c, first):
        block = held[b, c]

        def one(i, carry):
            at = pl.ds(pl.multiple_of(i * 256, 256), 256)
            value = lax.dot_general(
                source[c, at, :], block, (((1,), (1,)), ((), ())),
                preferred_element_type=jnp.float32,
            )

            @pl.when(c == first)
            def _():
                acc[at, :] = value

            @pl.when(c != first)
            def _():
                acc[at, :] += value

            return carry

        lax.fori_loop(0, rows // 256, one, 0)

    def part_copy(b, d):
        return pltpu.make_async_remote_copy(
            src_ref=part_buf.at[d - 1, b],
            dst_ref=got_hbm.at[d - 1, :, pl.ds(pl.multiple_of(b * width, width), width)],
            send_sem=part_send.at[d - 1, b], recv_sem=part_recv.at[d - 1, b],
            device_id={"dim": lax.rem(x + d, nd)}, device_id_type=MESH,
        )

    def own_copy(b):
        return pltpu.make_async_copy(
            out_buf.at[b],
            own_hbm.at[:, pl.ds(pl.multiple_of(b * width, width), width)],
            own_sem.at[b],
        )

    def end_copy(b, d):
        return pltpu.make_async_remote_copy(
            src_ref=end_part.at[d - 1, b], dst_ref=end_got.at[d - 1, b],
            send_sem=end_send.at[d - 1, b], recv_sem=end_recv.at[d - 1, b],
            device_id={"dim": lax.rem(x + d, nd)}, device_id_type=MESH,
        )

    def back_copy(b, to):
        return pltpu.make_async_remote_copy(
            src_ref=end_sum.at[b], dst_ref=back.at[b],
            send_sem=back_send.at[b], recv_sem=back_recv.at[b],
            device_id={"blk": to}, device_id_type=MESH,
        )

    def tile_keep(i, b):
        return keep[x * (half // tile) + i, b].astype(jnp.float32)

    def masked(acc, b, first):
        values = []
        for i in range(half // tile):
            t = first * (half // tile) + i
            at = pl.ds(pl.multiple_of(t * tile, tile), tile)
            values.append(acc[at, :] * keep[t, b].astype(jnp.float32))
        return values

    def finish(acc, b):
        for d in range(1, nd):
            for i, value in enumerate(masked(acc, b, lax.rem(x + d, nd))):
                part_buf[d - 1, b, i * tile : (i + 1) * tile, :] = value.astype(jnp.bfloat16)
            part_copy(b, d).start()
        for i, value in enumerate(masked(acc, b, x)):
            out_buf[b, i * tile : (i + 1) * tile, :] = value

        @pl.when(between | (b == z))
        def _():
            own_copy(b).start()

    @pl.when(between)
    def _():
        for c in range(lent):
            load(c).wait()

    for c in range(lent, chunks):
        load(c).wait()

    def own_chunk(c, carry):
        add_chunk(acc_hi, train, z, c, 0)
        return carry

    lax.fori_loop(0, chunks, own_chunk, 0)
    finish(acc_hi, z)

    def half_of(owner):
        return pl.ds(pl.multiple_of(owner * half, half), half)

    def help_end():
        for c in range(lent):
            slice_copy(c).wait_recv()
            for d in range(1, nr):
                twin_copy(c, d, r).start()
        for c in range(lent):
            for d in range(1, nr):
                twin_copy(c, d, lax.rem(r + d, nr)).wait_recv()

        def one_block(b, carry):
            @pl.when(b != outer)
            def _():
                def one_chunk(c, carry):
                    add_chunk(acc_off, end_train, b, c, 0)
                    return carry

                lax.fori_loop(0, lent, one_chunk, 0)
                for d in range(1, nd):
                    end_part[d - 1, b] = acc_off[half_of(lax.rem(x + d, nd)), :].astype(jnp.bfloat16)
                    end_copy(b, d).start()
                end_own[b] = acc_off[half_of(x), :]

            return carry

        lax.fori_loop(0, nb, one_block, 0)

    first_far = jnp.where(is_end, lent, 0)

    def step(s, carry):
        hi = jnp.where(hi_host & (s == 2), nb - 1, z + s)
        lo = jnp.where(lo_host & (s == 2), 0, z - s)
        has_a = hi < nb
        has_b = lo >= 0

        def chunk(c, carry):
            early = c < lent
            turn = (early & (s == 1)) | (jnp.logical_not(early) & (s == 2))
            take_hi = has_a & (has_lo | jnp.logical_not(early)) & (jnp.logical_not(hi_host) | turn)
            take_lo = has_b & (has_hi | jnp.logical_not(early)) & (jnp.logical_not(lo_host) | turn)

            @pl.when(is_host & (s == nb - 2) & (c == lent))
            def _():
                help_end()

            @pl.when(take_hi)
            def _():
                to_lo(hi, c).wait_recv()

                @pl.when(goes_lo(c))
                def _():
                    to_lo(hi, c).start()

            @pl.when(take_lo)
            def _():
                to_hi(lo, c).wait_recv()

                @pl.when(goes_hi(c))
                def _():
                    to_hi(lo, c).start()

            @pl.when(take_hi)
            def _():
                add_chunk(acc_hi, train, hi, c, first_far)

            @pl.when(take_lo)
            def _():
                add_chunk(acc_lo, train, lo, c, first_far)

            return carry

        lax.fori_loop(0, chunks, chunk, 0)

        @pl.when(has_a & (jnp.logical_not(hi_host) | (s == 2)))
        def _():
            finish(acc_hi, hi)

        @pl.when(has_b & (jnp.logical_not(lo_host) | (s == 2)))
        def _():
            finish(acc_lo, lo)

        return carry

    lax.fori_loop(1, nb, step, 0)

    @pl.when(is_host)
    def _():
        def one_block(b, carry):
            @pl.when(b != outer)
            def _():
                for d in range(1, nd):
                    end_copy(b, d).wait_recv()
                value = end_own[b]
                for d in range(1, nd):
                    value += end_got[d - 1, b].astype(jnp.float32)
                end_sum[b] = value.astype(jnp.bfloat16)
                back_copy(b, outer).start()

            return carry

        lax.fori_loop(0, nb, one_block, 0)

    @pl.when(is_end)
    def _():
        def one_block(k, carry):
            b = jnp.where(has_lo, k, nb - 1 - k)

            @pl.when(b != z)
            def _():
                back_copy(b, host).wait_recv()
                for i in range(half // tile):
                    at = slice(i * tile, (i + 1) * tile)
                    out_buf[b, at, :] += back[b, at, :].astype(jnp.float32) * tile_keep(i, b)
                own_copy(b).start()

            return carry

        lax.fori_loop(0, nb, one_block, 0)

    def drain(b, carry):
        def drain_chunk(c, carry):
            @pl.when(goes_lo(c) & (b >= z))
            def _():
                to_lo(b, c).wait_send()

            @pl.when(goes_hi(c) & (b <= z))
            def _():
                to_hi(b, c).wait_send()

            return carry

        lax.fori_loop(0, chunks, drain_chunk, 0)
        own_copy(b).wait()
        for d in range(1, nd):
            part_copy(b, d).wait()

        @pl.when(is_host & (b != outer))
        def _():
            for d in range(1, nd):
                end_copy(b, d).wait_send()
            back_copy(b, outer).wait_send()

        return carry

    lax.fori_loop(0, nb, drain, 0)

    @pl.when(is_end)
    def _():
        for c in range(lent):
            slice_copy(c).wait_send()

    @pl.when(is_host)
    def _():
        for c in range(lent):
            for d in range(1, nr):
                twin_copy(c, d, r).wait_send()


def body(train_grads, query_grads, precond, candidates):
    rows, depth = train_grads.shape
    width = query_grads.shape[0]
    nb, nd, nr = (lax.axis_size(name) for name in ("blk", "dim", "rep"))
    chunks, lent = 8, 2
    half = rows // nd
    own, got = pl.pallas_call(
        functools.partial(kernel, nb, nd, nr),
        out_shape=(
            jax.ShapeDtypeStruct((half, nb * width), jnp.float32),
            jax.ShapeDtypeStruct((nd - 1, half, nb * width), jnp.bfloat16),
        ),
        in_specs=[
            pl.BlockSpec(memory_space=pltpu.VMEM),
            pl.BlockSpec(memory_space=pltpu.VMEM),
            pl.BlockSpec(memory_space=pltpu.SMEM),
            pl.BlockSpec(memory_space=pl.ANY),
        ],
        out_specs=(pl.BlockSpec(memory_space=pl.ANY), pl.BlockSpec(memory_space=pl.ANY)),
        scratch_shapes=[
            pltpu.VMEM((chunks, rows, depth // chunks), jnp.bfloat16),
            pltpu.VMEM((nb, chunks, width, depth // chunks), jnp.bfloat16),
            pltpu.VMEM((rows, width), jnp.float32),
            pltpu.VMEM((rows, width), jnp.float32),
            pltpu.VMEM((rows, width), jnp.float32),
            pltpu.VMEM((nb, half, width), jnp.float32),
            pltpu.VMEM((nd - 1, nb, half, width), jnp.bfloat16),
            pltpu.VMEM((lent, rows, depth // chunks), jnp.bfloat16),
            pltpu.VMEM((nb, half, width), jnp.float32),
            pltpu.VMEM((nd - 1, nb, half, width), jnp.bfloat16),
            pltpu.VMEM((nd - 1, nb, half, width), jnp.bfloat16),
            pltpu.VMEM((nb, half, width), jnp.bfloat16),
            pltpu.VMEM((nb, half, width), jnp.bfloat16),
            pltpu.SemaphoreType.DMA((chunks,)),
            pltpu.SemaphoreType.DMA((nb, chunks)),
            pltpu.SemaphoreType.DMA((nb, chunks)),
            pltpu.SemaphoreType.DMA((nb, chunks)),
            pltpu.SemaphoreType.DMA((nd - 1, nb)),
            pltpu.SemaphoreType.DMA((nd - 1, nb)),
            pltpu.SemaphoreType.DMA((nb,)),
            pltpu.SemaphoreType.DMA((lent,)),
            pltpu.SemaphoreType.DMA((lent, nr)),
            pltpu.SemaphoreType.DMA((lent, nr)),
            pltpu.SemaphoreType.DMA((nd - 1, nb)),
            pltpu.SemaphoreType.DMA((nd - 1, nb)),
            pltpu.SemaphoreType.DMA((nb,)),
            pltpu.SemaphoreType.DMA((nb,)),
        ],
        compiler_params=pltpu.CompilerParams(
            collective_id=0, has_side_effects=True, vmem_limit_bytes=44 * 2**20
        ),
    )(query_grads, precond[None, :], candidates, train_grads)
    total = own
    for d in range(nd - 1):
        total = total + got[d].astype(jnp.float32)
    return total


def solution(mesh):
    in_specs = (
        P(("groups", "blk"), "dim"),
        P(("groups", "rep", "blk"), "dim"),
        P("dim"),
        P(("groups", "blk"), "rep"),
    )
    out_specs = P(("groups", "blk", "dim"), "rep")
    return jax.shard_map(body, mesh=mesh, in_specs=in_specs, out_specs=out_specs, check_vma=False)
```

```python
import functools

import jax
import jax.numpy as jnp
from jax import lax
from jax.experimental import pallas as pl
from jax.experimental.pallas import tpu as pltpu
from jax.sharding import PartitionSpec as P

MESH = pl.DeviceIdType.MESH


def kernel(
    nb, nd, nr, lag, query, precond, keep, train_hbm, own_hbm, got_hbm,
    train, held, acc_hi, acc_lo, acc_off, out_buf, part_buf,
    end_train, end_own, end_part, end_got, end_sum, back,
    train_sem, send_lo, send_hi, recv, part_send, part_recv, own_sem,
    slice_send, slice_recv, twin_send, end_send, end_recv, back_send, back_recv,
):
    chunks, rows, depth = train.shape
    lent = end_train.shape[0]
    width = held.shape[2]
    half = rows // nd
    share = rows // nr
    tiles = keep.shape[0]
    tile = rows // tiles
    z = lax.axis_index("blk")
    x = lax.axis_index("dim")
    r = lax.axis_index("rep")
    has_lo = z > 0
    has_hi = z < nb - 1
    between = has_lo & has_hi
    is_end = jnp.logical_not(between)
    lo_host, hi_host = z == 1, z == nb - 2
    is_host = lo_host | hi_host
    outer = jnp.where(lo_host, 0, nb - 1)
    host = jnp.where(has_lo, nb - 2, 1)
    barrier = pltpu.get_barrier_semaphore()

    @pl.when(has_lo)
    def _():
        pl.semaphore_signal(barrier, inc=1, device_id={"blk": z - 1}, device_id_type=MESH)

    @pl.when(has_hi)
    def _():
        pl.semaphore_signal(barrier, inc=1, device_id={"blk": z + 1}, device_id_type=MESH)

    for d in range(1, nd):
        pl.semaphore_signal(
            barrier, inc=1, device_id={"dim": lax.rem(x + d, nd)}, device_id_type=MESH
        )
    for d in range(1, nr):
        pl.semaphore_signal(
            barrier, inc=1, device_id={"rep": lax.rem(r + d, nr)}, device_id_type=MESH
        )

    def load(c):
        return pltpu.make_async_copy(
            train_hbm.at[:, pl.ds(c * depth, depth)], train.at[c], train_sem.at[c]
        )

    for c in range(chunks):
        load(c).start()

    def to_lo(b, c):
        return pltpu.make_async_remote_copy(
            src_ref=held.at[b, c], dst_ref=held.at[b, c],
            send_sem=send_lo.at[b, c], recv_sem=recv.at[b, c],
            device_id={"blk": z - 1}, device_id_type=MESH,
        )

    def to_hi(b, c):
        return pltpu.make_async_remote_copy(
            src_ref=held.at[b, c], dst_ref=held.at[b, c],
            send_sem=send_hi.at[b, c], recv_sem=recv.at[b, c],
            device_id={"blk": z + 1}, device_id_type=MESH,
        )

    def goes_lo(c):
        return has_lo & ((z > 1) | (c >= lent))

    def goes_hi(c):
        return has_hi & ((z < nb - 2) | (c >= lent))

    def share_of(owner):
        return pl.ds(pl.multiple_of(owner * share, share), share)

    def slice_copy(c):
        return pltpu.make_async_remote_copy(
            src_ref=train.at[c, share_of(r), :], dst_ref=end_train.at[c, share_of(r), :],
            send_sem=slice_send.at[c], recv_sem=slice_recv.at[c, r],
            device_id={"blk": host}, device_id_type=MESH,
        )

    def twin_copy(c, d, owner):
        return pltpu.make_async_remote_copy(
            src_ref=end_train.at[c, share_of(owner), :],
            dst_ref=end_train.at[c, share_of(owner), :],
            send_sem=twin_send.at[c, d - 1], recv_sem=slice_recv.at[c, owner],
            device_id={"rep": lax.rem(r + d, nr)}, device_id_type=MESH,
        )

    def prepare(c):
        span = slice(c * depth, (c + 1) * depth)
        scale = lax.rsqrt(precond[:, span])
        held[z, c] = (query[:, span].astype(jnp.float32) * scale).astype(jnp.bfloat16)

    prepare(0)

    @pl.when(between)
    def _():
        pl.semaphore_wait(barrier, nd + nr)

    @pl.when(is_end)
    def _():
        pl.semaphore_wait(barrier, nd + nr - 1)

    for c in range(chunks):
        if c:
            prepare(c)
        if c == lent:

            @pl.when(is_end)
            def _():
                for e in range(lent):
                    load(e).wait()
                    slice_copy(e).start()

        @pl.when(goes_lo(c))
        def _():
            to_lo(z, c).start()

        @pl.when(goes_hi(c))
        def _():
            to_hi(z, c).start()

    def add_chunk(acc, source, b, c, first):
        block = held[b, c]

        value = lax.dot_general(
            source[c], block, (((1,), (1,)), ((), ())), preferred_element_type=jnp.float32
        )

        @pl.when(c == first)
        def _():
            acc[...] = value

        @pl.when(c != first)
        def _():
            acc[...] += value

    def part_copy(b, d):
        return pltpu.make_async_remote_copy(
            src_ref=part_buf.at[d - 1, b],
            dst_ref=got_hbm.at[d - 1, :, pl.ds(pl.multiple_of(b * width, width), width)],
            send_sem=part_send.at[d - 1, b], recv_sem=part_recv.at[d - 1, b],
            device_id={"dim": lax.rem(x + d, nd)}, device_id_type=MESH,
        )

    def own_copy(b):
        return pltpu.make_async_copy(
            out_buf.at[b],
            own_hbm.at[:, pl.ds(pl.multiple_of(b * width, width), width)],
            own_sem.at[b],
        )

    def end_copy(b, d):
        return pltpu.make_async_remote_copy(
            src_ref=end_part.at[d - 1, b], dst_ref=end_got.at[d - 1, b],
            send_sem=end_send.at[d - 1, b], recv_sem=end_recv.at[d - 1, b],
            device_id={"dim": lax.rem(x + d, nd)}, device_id_type=MESH,
        )

    def back_copy(b, to):
        return pltpu.make_async_remote_copy(
            src_ref=end_sum.at[b], dst_ref=back.at[b],
            send_sem=back_send.at[b], recv_sem=back_recv.at[b],
            device_id={"blk": to}, device_id_type=MESH,
        )

    def tile_keep(i, b):
        return keep[x * (half // tile) + i, b].astype(jnp.float32)

    def masked(acc, b, first):
        values = []
        for i in range(half // tile):
            t = first * (half // tile) + i
            at = pl.ds(pl.multiple_of(t * tile, tile), tile)
            values.append(acc[at, :] * keep[t, b].astype(jnp.float32))
        return values

    def finish(acc, b):
        for d in range(1, nd):
            for i, value in enumerate(masked(acc, b, lax.rem(x + d, nd))):
                part_buf[d - 1, b, i * tile : (i + 1) * tile, :] = value.astype(jnp.bfloat16)
            part_copy(b, d).start()
        for i, value in enumerate(masked(acc, b, x)):
            out_buf[b, i * tile : (i + 1) * tile, :] = value

        @pl.when(between | (b == z))
        def _():
            own_copy(b).start()

    @pl.when(between)
    def _():
        for c in range(lent):
            load(c).wait()

    for c in range(lent, chunks):
        load(c).wait()

    def own_chunk(c, carry):
        add_chunk(acc_hi, train, z, c, 0)
        return carry

    lax.fori_loop(0, chunks, own_chunk, 0)
    finish(acc_hi, z)

    def half_of(owner):
        return pl.ds(pl.multiple_of(owner * half, half), half)

    def help_end():
        for c in range(lent):
            slice_copy(c).wait_recv()
            for d in range(1, nr):
                twin_copy(c, d, r).start()
        for c in range(lent):
            for d in range(1, nr):
                twin_copy(c, d, lax.rem(r + d, nr)).wait_recv()

        def one_block(b, carry):
            @pl.when(b != outer)
            def _():
                def one_chunk(c, carry):
                    add_chunk(acc_off, end_train, b, c, 0)
                    return carry

                lax.fori_loop(0, lent, one_chunk, 0)
                for d in range(1, nd):
                    end_part[d - 1, b] = acc_off[half_of(lax.rem(x + d, nd)), :].astype(jnp.bfloat16)
                    end_copy(b, d).start()
                end_own[b] = acc_off[half_of(x), :]

            return carry

        lax.fori_loop(0, nb, one_block, 0)

    first_far = jnp.where(is_end, lent, 0)

    def step(s, carry):
        hi = jnp.where(hi_host & (s == 2), nb - 1, z + s)
        lo = jnp.where(lo_host & (s == 2), 0, z - s)
        has_a = hi < nb
        has_b = lo >= 0

        second = is_host & (s == 2)

        def chunk(i, carry):
            late = second & (i >= lent)
            inner_c = jnp.where(late, i - lag, i)
            inner_ok = (inner_c < chunks) & (jnp.logical_not(late) | (i >= lent + lag))
            outer_c = jnp.where(s == 1, i - (chunks - lent), i)
            outer_ok = (outer_c < chunks) & (
                ((s == 1) & (outer_c >= 0) & (outer_c < lent)) | ((s == 2) & (outer_c >= lent))
            )
            hi_c = jnp.where(hi_host, outer_c, inner_c)
            lo_c = jnp.where(lo_host, outer_c, inner_c)
            hi_ok = (hi_host & outer_ok) | (jnp.logical_not(hi_host) & inner_ok)
            lo_ok = (lo_host & outer_ok) | (jnp.logical_not(lo_host) & inner_ok)
            take_hi = has_a & hi_ok & (has_lo | (hi_c >= lent))
            take_lo = has_b & lo_ok & (has_hi | (lo_c >= lent))

            @pl.when(is_host & (s == nb - 2) & (i == lent))
            def _():
                help_end()

            @pl.when(take_hi)
            def _():
                to_lo(hi, hi_c).wait_recv()

                @pl.when(goes_lo(hi_c))
                def _():
                    to_lo(hi, hi_c).start()

            @pl.when(take_lo)
            def _():
                to_hi(lo, lo_c).wait_recv()

                @pl.when(goes_hi(lo_c))
                def _():
                    to_hi(lo, lo_c).start()

            @pl.when(take_hi)
            def _():
                add_chunk(acc_hi, train, hi, hi_c, first_far)

            @pl.when(take_lo)
            def _():
                add_chunk(acc_lo, train, lo, lo_c, first_far)

            return carry

        lax.fori_loop(0, chunks + lag, chunk, 0)

        @pl.when(has_a & (jnp.logical_not(hi_host) | (s == 2)))
        def _():
            finish(acc_hi, hi)

        @pl.when(has_b & (jnp.logical_not(lo_host) | (s == 2)))
        def _():
            finish(acc_lo, lo)

        return carry

    lax.fori_loop(1, nb, step, 0)

    @pl.when(is_host)
    def _():
        def one_block(b, carry):
            @pl.when(b != outer)
            def _():
                for d in range(1, nd):
                    end_copy(b, d).wait_recv()
                value = end_own[b]
                for d in range(1, nd):
                    value += end_got[d - 1, b].astype(jnp.float32)
                end_sum[b] = value.astype(jnp.bfloat16)
                back_copy(b, outer).start()

            return carry

        lax.fori_loop(0, nb, one_block, 0)

    @pl.when(is_end)
    def _():
        def one_block(k, carry):
            b = jnp.where(has_lo, k, nb - 1 - k)

            @pl.when(b != z)
            def _():
                back_copy(b, host).wait_recv()
                for i in range(half // tile):
                    at = slice(i * tile, (i + 1) * tile)
                    out_buf[b, at, :] += back[b, at, :].astype(jnp.float32) * tile_keep(i, b)
                own_copy(b).start()

            return carry

        lax.fori_loop(0, nb, one_block, 0)

    def drain(b, carry):
        def drain_chunk(c, carry):
            @pl.when(goes_lo(c) & (b >= z))
            def _():
                to_lo(b, c).wait_send()

            @pl.when(goes_hi(c) & (b <= z))
            def _():
                to_hi(b, c).wait_send()

            return carry

        lax.fori_loop(0, chunks, drain_chunk, 0)
        own_copy(b).wait()
        for d in range(1, nd):
            part_copy(b, d).wait()

        @pl.when(is_host & (b != outer))
        def _():
            for d in range(1, nd):
                end_copy(b, d).wait_send()
            back_copy(b, outer).wait_send()

        return carry

    lax.fori_loop(0, nb, drain, 0)

    @pl.when(is_end)
    def _():
        for c in range(lent):
            slice_copy(c).wait_send()

    @pl.when(is_host)
    def _():
        for c in range(lent):
            for d in range(1, nr):
                twin_copy(c, d, r).wait_send()


def body(train_grads, query_grads, precond, candidates):
    rows, depth = train_grads.shape
    width = query_grads.shape[0]
    nb, nd, nr = (lax.axis_size(name) for name in ("blk", "dim", "rep"))
    chunks, lent, lag = 8, 2, 2
    half = rows // nd
    own, got = pl.pallas_call(
        functools.partial(kernel, nb, nd, nr, lag),
        out_shape=(
            jax.ShapeDtypeStruct((half, nb * width), jnp.float32),
            jax.ShapeDtypeStruct((nd - 1, half, nb * width), jnp.bfloat16),
        ),
        in_specs=[
            pl.BlockSpec(memory_space=pltpu.VMEM),
            pl.BlockSpec(memory_space=pltpu.VMEM),
            pl.BlockSpec(memory_space=pltpu.SMEM),
            pl.BlockSpec(memory_space=pl.ANY),
        ],
        out_specs=(pl.BlockSpec(memory_space=pl.ANY), pl.BlockSpec(memory_space=pl.ANY)),
        scratch_shapes=[
            pltpu.VMEM((chunks, rows, depth // chunks), jnp.bfloat16),
            pltpu.VMEM((nb, chunks, width, depth // chunks), jnp.bfloat16),
            pltpu.VMEM((rows, width), jnp.float32),
            pltpu.VMEM((rows, width), jnp.float32),
            pltpu.VMEM((rows, width), jnp.float32),
            pltpu.VMEM((nb, half, width), jnp.float32),
            pltpu.VMEM((nd - 1, nb, half, width), jnp.bfloat16),
            pltpu.VMEM((lent, rows, depth // chunks), jnp.bfloat16),
            pltpu.VMEM((nb, half, width), jnp.float32),
            pltpu.VMEM((nd - 1, nb, half, width), jnp.bfloat16),
            pltpu.VMEM((nd - 1, nb, half, width), jnp.bfloat16),
            pltpu.VMEM((nb, half, width), jnp.bfloat16),
            pltpu.VMEM((nb, half, width), jnp.bfloat16),
            pltpu.SemaphoreType.DMA((chunks,)),
            pltpu.SemaphoreType.DMA((nb, chunks)),
            pltpu.SemaphoreType.DMA((nb, chunks)),
            pltpu.SemaphoreType.DMA((nb, chunks)),
            pltpu.SemaphoreType.DMA((nd - 1, nb)),
            pltpu.SemaphoreType.DMA((nd - 1, nb)),
            pltpu.SemaphoreType.DMA((nb,)),
            pltpu.SemaphoreType.DMA((lent,)),
            pltpu.SemaphoreType.DMA((lent, nr)),
            pltpu.SemaphoreType.DMA((lent, nr)),
            pltpu.SemaphoreType.DMA((nd - 1, nb)),
            pltpu.SemaphoreType.DMA((nd - 1, nb)),
            pltpu.SemaphoreType.DMA((nb,)),
            pltpu.SemaphoreType.DMA((nb,)),
        ],
        compiler_params=pltpu.CompilerParams(
            collective_id=0, has_side_effects=True, vmem_limit_bytes=44 * 2**20
        ),
    )(query_grads, precond[None, :], candidates, train_grads)
    total = own
    for d in range(nd - 1):
        total = total + got[d].astype(jnp.float32)
    return total


def solution(mesh):
    in_specs = (
        P(("groups", "blk"), "dim"),
        P(("groups", "rep", "blk"), "dim"),
        P("dim"),
        P(("groups", "blk"), "rep"),
    )
    out_specs = P(("groups", "blk", "dim"), "rep")
    return jax.shard_map(body, mesh=mesh, in_specs=in_specs, out_specs=out_specs, check_vma=False)
```

```python
import functools

import jax
import jax.numpy as jnp
from jax import lax
from jax.experimental import pallas as pl
from jax.experimental.pallas import tpu as pltpu
from jax.sharding import PartitionSpec as P

MESH = pl.DeviceIdType.MESH


def kernel(
    nb, nd, nr, lag, query, precond, keep, train_hbm, own_hbm, got_hbm,
    train, held, acc_hi, acc_lo, acc_off, out_buf, part_buf,
    end_train, end_own, end_part, end_got, end_sum, back,
    train_sem, send_lo, send_hi, recv, part_send, part_recv, own_sem,
    slice_send, slice_recv, twin_send, end_send, end_recv, back_send, back_recv,
):
    chunks, rows, depth = train.shape
    lent = end_train.shape[0]
    width = held.shape[2]
    half = rows // nd
    share = rows // nr
    tiles = keep.shape[0]
    tile = rows // tiles
    z = lax.axis_index("blk")
    x = lax.axis_index("dim")
    r = lax.axis_index("rep")
    has_lo = z > 0
    has_hi = z < nb - 1
    between = has_lo & has_hi
    is_end = jnp.logical_not(between)
    lo_host, hi_host = z == 1, z == nb - 2
    is_host = lo_host | hi_host
    outer = jnp.where(lo_host, 0, nb - 1)
    host = jnp.where(has_lo, nb - 2, 1)
    barrier = pltpu.get_barrier_semaphore()

    @pl.when(has_lo)
    def _():
        pl.semaphore_signal(barrier, inc=1, device_id={"blk": z - 1}, device_id_type=MESH)

    @pl.when(has_hi)
    def _():
        pl.semaphore_signal(barrier, inc=1, device_id={"blk": z + 1}, device_id_type=MESH)

    for d in range(1, nd):
        pl.semaphore_signal(
            barrier, inc=1, device_id={"dim": lax.rem(x + d, nd)}, device_id_type=MESH
        )
    for d in range(1, nr):
        pl.semaphore_signal(
            barrier, inc=1, device_id={"rep": lax.rem(r + d, nr)}, device_id_type=MESH
        )

    def load(c):
        return pltpu.make_async_copy(
            train_hbm.at[:, pl.ds(c * depth, depth)], train.at[c], train_sem.at[c]
        )

    for c in range(chunks):
        load(c).start()

    def to_lo(b, c):
        return pltpu.make_async_remote_copy(
            src_ref=held.at[b, c], dst_ref=held.at[b, c],
            send_sem=send_lo.at[b, c], recv_sem=recv.at[b, c],
            device_id={"blk": z - 1}, device_id_type=MESH,
        )

    def to_hi(b, c):
        return pltpu.make_async_remote_copy(
            src_ref=held.at[b, c], dst_ref=held.at[b, c],
            send_sem=send_hi.at[b, c], recv_sem=recv.at[b, c],
            device_id={"blk": z + 1}, device_id_type=MESH,
        )

    def goes_lo(c):
        return has_lo & ((z > 1) | (c >= lent))

    def goes_hi(c):
        return has_hi & ((z < nb - 2) | (c >= lent))

    def share_of(owner):
        return pl.ds(pl.multiple_of(owner * share, share), share)

    def slice_copy(c):
        return pltpu.make_async_remote_copy(
            src_ref=train.at[c, share_of(r), :], dst_ref=end_train.at[c, share_of(r), :],
            send_sem=slice_send.at[c], recv_sem=slice_recv.at[c, r],
            device_id={"blk": host}, device_id_type=MESH,
        )

    def twin_copy(c, d, owner):
        return pltpu.make_async_remote_copy(
            src_ref=end_train.at[c, share_of(owner), :],
            dst_ref=end_train.at[c, share_of(owner), :],
            send_sem=twin_send.at[c, d - 1], recv_sem=slice_recv.at[c, owner],
            device_id={"rep": lax.rem(r + d, nr)}, device_id_type=MESH,
        )

    def prepare(c):
        span = slice(c * depth, (c + 1) * depth)
        scale = lax.rsqrt(precond[:, span])
        held[z, c] = (query[:, span].astype(jnp.float32) * scale).astype(jnp.bfloat16)

    prepare(0)

    @pl.when(between)
    def _():
        pl.semaphore_wait(barrier, nd + nr)

    @pl.when(is_end)
    def _():
        pl.semaphore_wait(barrier, nd + nr - 1)

    for c in range(chunks):
        if c:
            prepare(c)
        if c == 1:

            @pl.when(is_end)
            def _():
                for e in range(lent):
                    load(e).wait()
                    slice_copy(e).start()

        @pl.when(goes_lo(c))
        def _():
            to_lo(z, c).start()

        @pl.when(goes_hi(c))
        def _():
            to_hi(z, c).start()

    def add_chunk(acc, source, b, c, first):
        block = held[b, c]

        value = lax.dot_general(
            source[c], block, (((1,), (1,)), ((), ())), preferred_element_type=jnp.float32
        )

        @pl.when(c == first)
        def _():
            acc[...] = value

        @pl.when(c != first)
        def _():
            acc[...] += value

    def part_copy(b, d):
        return pltpu.make_async_remote_copy(
            src_ref=part_buf.at[d - 1, b],
            dst_ref=got_hbm.at[d - 1, :, pl.ds(pl.multiple_of(b * width, width), width)],
            send_sem=part_send.at[d - 1, b], recv_sem=part_recv.at[d - 1, b],
            device_id={"dim": lax.rem(x + d, nd)}, device_id_type=MESH,
        )

    def own_copy(b):
        return pltpu.make_async_copy(
            out_buf.at[b],
            own_hbm.at[:, pl.ds(pl.multiple_of(b * width, width), width)],
            own_sem.at[b],
        )

    def end_copy(b, d):
        return pltpu.make_async_remote_copy(
            src_ref=end_part.at[d - 1, b], dst_ref=end_got.at[d - 1, b],
            send_sem=end_send.at[d - 1, b], recv_sem=end_recv.at[d - 1, b],
            device_id={"dim": lax.rem(x + d, nd)}, device_id_type=MESH,
        )

    def back_copy(b, to):
        return pltpu.make_async_remote_copy(
            src_ref=end_sum.at[b], dst_ref=back.at[b],
            send_sem=back_send.at[b], recv_sem=back_recv.at[b],
            device_id={"blk": to}, device_id_type=MESH,
        )

    def tile_keep(i, b):
        return keep[x * (half // tile) + i, b].astype(jnp.float32)

    def masked(acc, b, first):
        values = []
        for i in range(half // tile):
            t = first * (half // tile) + i
            at = pl.ds(pl.multiple_of(t * tile, tile), tile)
            values.append(acc[at, :] * keep[t, b].astype(jnp.float32))
        return values

    def finish(acc, b):
        for d in range(1, nd):
            for i, value in enumerate(masked(acc, b, lax.rem(x + d, nd))):
                part_buf[d - 1, b, i * tile : (i + 1) * tile, :] = value.astype(jnp.bfloat16)
            part_copy(b, d).start()
        for i, value in enumerate(masked(acc, b, x)):
            out_buf[b, i * tile : (i + 1) * tile, :] = value

        @pl.when(between | (b == z))
        def _():
            own_copy(b).start()

    @pl.when(between)
    def _():
        for c in range(lent):
            load(c).wait()

    for c in range(lent, chunks):
        load(c).wait()

    def own_chunk(c, carry):
        add_chunk(acc_hi, train, z, c, 0)
        return carry

    lax.fori_loop(0, chunks, own_chunk, 0)
    finish(acc_hi, z)

    def half_of(owner):
        return pl.ds(pl.multiple_of(owner * half, half), half)

    def help_end():
        for c in range(lent):
            slice_copy(c).wait_recv()
            for d in range(1, nr):
                twin_copy(c, d, r).start()
        for c in range(lent):
            for d in range(1, nr):
                twin_copy(c, d, lax.rem(r + d, nr)).wait_recv()

        def one_block(b, carry):
            @pl.when(b != outer)
            def _():
                def one_chunk(c, carry):
                    add_chunk(acc_off, end_train, b, c, 0)
                    return carry

                lax.fori_loop(0, lent, one_chunk, 0)
                for d in range(1, nd):
                    end_part[d - 1, b] = acc_off[half_of(lax.rem(x + d, nd)), :].astype(jnp.bfloat16)
                    end_copy(b, d).start()
                end_own[b] = acc_off[half_of(x), :]

            return carry

        lax.fori_loop(0, nb, one_block, 0)

    first_far = jnp.where(is_end, lent, 0)

    def step(s, carry):
        hi = jnp.where(hi_host & (s == 2), nb - 1, z + s)
        lo = jnp.where(lo_host & (s == 2), 0, z - s)
        has_a = hi < nb
        has_b = lo >= 0

        second = is_host & (s == 2)

        def chunk(i, carry):
            late = second & (i >= lent)
            inner_c = jnp.where(late, i - lag, i)
            inner_ok = (inner_c < chunks) & (jnp.logical_not(late) | (i >= lent + lag))
            outer_c = jnp.where(s == 1, i - (chunks - lent), i)
            outer_ok = (outer_c < chunks) & (
                ((s == 1) & (outer_c >= 0) & (outer_c < lent)) | ((s == 2) & (outer_c >= lent))
            )
            hi_c = jnp.where(hi_host, outer_c, inner_c)
            lo_c = jnp.where(lo_host, outer_c, inner_c)
            hi_ok = (hi_host & outer_ok) | (jnp.logical_not(hi_host) & inner_ok)
            lo_ok = (lo_host & outer_ok) | (jnp.logical_not(lo_host) & inner_ok)
            take_hi = has_a & hi_ok & (has_lo | (hi_c >= lent))
            take_lo = has_b & lo_ok & (has_hi | (lo_c >= lent))

            @pl.when(is_host & (s == nb - 2) & (i == lent))
            def _():
                help_end()

            @pl.when(take_hi)
            def _():
                to_lo(hi, hi_c).wait_recv()

                @pl.when(goes_lo(hi_c))
                def _():
                    to_lo(hi, hi_c).start()

            @pl.when(take_lo)
            def _():
                to_hi(lo, lo_c).wait_recv()

                @pl.when(goes_hi(lo_c))
                def _():
                    to_hi(lo, lo_c).start()

            @pl.when(take_hi)
            def _():
                add_chunk(acc_hi, train, hi, hi_c, first_far)

            @pl.when(take_lo)
            def _():
                add_chunk(acc_lo, train, lo, lo_c, first_far)

            return carry

        lax.fori_loop(0, chunks + lag, chunk, 0)

        @pl.when(has_a & (jnp.logical_not(hi_host) | (s == 2)))
        def _():
            finish(acc_hi, hi)

        @pl.when(has_b & (jnp.logical_not(lo_host) | (s == 2)))
        def _():
            finish(acc_lo, lo)

        return carry

    lax.fori_loop(1, nb, step, 0)

    @pl.when(is_host)
    def _():
        def one_block(b, carry):
            @pl.when(b != outer)
            def _():
                for d in range(1, nd):
                    end_copy(b, d).wait_recv()
                value = end_own[b]
                for d in range(1, nd):
                    value += end_got[d - 1, b].astype(jnp.float32)
                end_sum[b] = value.astype(jnp.bfloat16)
                back_copy(b, outer).start()

            return carry

        lax.fori_loop(0, nb, one_block, 0)

    @pl.when(is_end)
    def _():
        def one_block(k, carry):
            b = jnp.where(has_lo, k, nb - 1 - k)

            @pl.when(b != z)
            def _():
                back_copy(b, host).wait_recv()
                for i in range(half // tile):
                    at = slice(i * tile, (i + 1) * tile)
                    out_buf[b, at, :] += back[b, at, :].astype(jnp.float32) * tile_keep(i, b)
                own_copy(b).start()

            return carry

        lax.fori_loop(0, nb, one_block, 0)

    def drain(b, carry):
        def drain_chunk(c, carry):
            @pl.when(goes_lo(c) & (b >= z))
            def _():
                to_lo(b, c).wait_send()

            @pl.when(goes_hi(c) & (b <= z))
            def _():
                to_hi(b, c).wait_send()

            return carry

        lax.fori_loop(0, chunks, drain_chunk, 0)
        own_copy(b).wait()
        for d in range(1, nd):
            part_copy(b, d).wait()

        @pl.when(is_host & (b != outer))
        def _():
            for d in range(1, nd):
                end_copy(b, d).wait_send()
            back_copy(b, outer).wait_send()

        return carry

    lax.fori_loop(0, nb, drain, 0)

    @pl.when(is_end)
    def _():
        for c in range(lent):
            slice_copy(c).wait_send()

    @pl.when(is_host)
    def _():
        for c in range(lent):
            for d in range(1, nr):
                twin_copy(c, d, r).wait_send()


def body(train_grads, query_grads, precond, candidates):
    rows, depth = train_grads.shape
    width = query_grads.shape[0]
    nb, nd, nr = (lax.axis_size(name) for name in ("blk", "dim", "rep"))
    chunks, lent, lag = 8, 2, 2
    half = rows // nd
    own, got = pl.pallas_call(
        functools.partial(kernel, nb, nd, nr, lag),
        out_shape=(
            jax.ShapeDtypeStruct((half, nb * width), jnp.float32),
            jax.ShapeDtypeStruct((nd - 1, half, nb * width), jnp.bfloat16),
        ),
        in_specs=[
            pl.BlockSpec(memory_space=pltpu.VMEM),
            pl.BlockSpec(memory_space=pltpu.VMEM),
            pl.BlockSpec(memory_space=pltpu.SMEM),
            pl.BlockSpec(memory_space=pl.ANY),
        ],
        out_specs=(pl.BlockSpec(memory_space=pl.ANY), pl.BlockSpec(memory_space=pl.ANY)),
        scratch_shapes=[
            pltpu.VMEM((chunks, rows, depth // chunks), jnp.bfloat16),
            pltpu.VMEM((nb, chunks, width, depth // chunks), jnp.bfloat16),
            pltpu.VMEM((rows, width), jnp.float32),
            pltpu.VMEM((rows, width), jnp.float32),
            pltpu.VMEM((rows, width), jnp.float32),
            pltpu.VMEM((nb, half, width), jnp.float32),
            pltpu.VMEM((nd - 1, nb, half, width), jnp.bfloat16),
            pltpu.VMEM((lent, rows, depth // chunks), jnp.bfloat16),
            pltpu.VMEM((nb, half, width), jnp.float32),
            pltpu.VMEM((nd - 1, nb, half, width), jnp.bfloat16),
            pltpu.VMEM((nd - 1, nb, half, width), jnp.bfloat16),
            pltpu.VMEM((nb, half, width), jnp.bfloat16),
            pltpu.VMEM((nb, half, width), jnp.bfloat16),
            pltpu.SemaphoreType.DMA((chunks,)),
            pltpu.SemaphoreType.DMA((nb, chunks)),
            pltpu.SemaphoreType.DMA((nb, chunks)),
            pltpu.SemaphoreType.DMA((nb, chunks)),
            pltpu.SemaphoreType.DMA((nd - 1, nb)),
            pltpu.SemaphoreType.DMA((nd - 1, nb)),
            pltpu.SemaphoreType.DMA((nb,)),
            pltpu.SemaphoreType.DMA((lent,)),
            pltpu.SemaphoreType.DMA((lent, nr)),
            pltpu.SemaphoreType.DMA((lent, nr)),
            pltpu.SemaphoreType.DMA((nd - 1, nb)),
            pltpu.SemaphoreType.DMA((nd - 1, nb)),
            pltpu.SemaphoreType.DMA((nb,)),
            pltpu.SemaphoreType.DMA((nb,)),
        ],
        compiler_params=pltpu.CompilerParams(
            collective_id=0, has_side_effects=True, vmem_limit_bytes=44 * 2**20
        ),
    )(query_grads, precond[None, :], candidates, train_grads)
    total = own
    for d in range(nd - 1):
        total = total + got[d].astype(jnp.float32)
    return total


def solution(mesh):
    in_specs = (
        P(("groups", "blk"), "dim"),
        P(("groups", "rep", "blk"), "dim"),
        P("dim"),
        P(("groups", "blk"), "rep"),
    )
    out_specs = P(("groups", "blk", "dim"), "rep")
    return jax.shard_map(body, mesh=mesh, in_specs=in_specs, out_specs=out_specs, check_vma=False)
```
